32 devices in a mesh: dp: 8 (over z, core), neuron: 4 (over y, x).
Axes of the slice: x: 2, y: 2, z: 4, core: 2. Of those that a mesh axis runs over, the one named last changes fastest.
Arguments:
- acts_a: bfloat16 [4096, 4096], P('dp'), may hold values from -150 to 150
- acts_b: bfloat16 [4096, 4096], P('dp'), may hold values from -150 to 150
- grads_a: bfloat16 [4096, 14336], P('dp', 'neuron'), may hold values from -150 to 150
- grads_b: bfloat16 [4096, 14336], P('dp', 'neuron'), may hold values from -150 to 150
- weights_a: bfloat16 [4096, 14336], P('dp', 'neuron'), may hold values from -6 to 6
- weights_b: bfloat16 [4096, 14336], P('dp', 'neuron'), may hold values from -6 to 6
- block_match: int32 [112], replicated, may hold values from 0 to 111, as said below
Outputs:
- merged: float32 [4096, 14336], P('dp', 'neuron')
The draws below stay inside these ranges and needn't reach their ends.
Inputs may be any that keep to these rules, and one draw needn't show every extreme that they name: `block_match`: A permutation of the 112 blocks. For any two indices s and t of neuron (s may equal t), at most 7 of the 28 blocks held by s is matched to a position held by t; so each index receives its 28 matched blocks from 28 different indices, one of them itself.
All inputs are finite; a program needn't handle non-finite values.
Results may differ from the reference program's by a relative error of at most 0.0003.
Values may be sent and summed in bfloat16 or wider, within the bound.
A program may use at most 256 MiB of HBM per device.

```python
import math
import jax
import jax.numpy as jnp
from jax import lax

D = 4096
FF = 14336
BLK = 128
TOK_DEV = 512
TOKENS = 4096
NBLK = 112
BL = 28
CAP = 7
N_DP = 8


def heavy(key, rows, cols):
    k_base, k_spread, k_row, k_col = jax.random.split(key, 4)
    base = jnp.clip(jax.random.normal(k_base, (rows, cols), jnp.float32), -4.0, 4.0)
    row_scale = jnp.exp(jax.random.uniform(k_row, (rows, 1), jnp.float32, math.log(0.3), math.log(3.0)))
    spread = jnp.exp(jax.random.uniform(k_spread, (rows, cols), jnp.float32, -1.2, 1.2))
    col_scale = jnp.exp(jax.random.uniform(k_col, (1, cols), jnp.float32, math.log(0.3), math.log(3.0)))
    return base * spread * row_scale * col_scale


def draw_acts_a(key, part):
    return heavy(jax.random.fold_in(key, 11), TOKENS, D).astype(jnp.bfloat16)


def draw_acts_b(key, part):
    return heavy(jax.random.fold_in(key, 12), TOKENS, D).astype(jnp.bfloat16)


def draw_grads_a(key, part):
    return heavy(jax.random.fold_in(key, 13), TOKENS, FF).astype(jnp.bfloat16)


def draw_grads_b(key, part):
    return heavy(jax.random.fold_in(key, 14), TOKENS, FF).astype(jnp.bfloat16)


def draw_block_match(key, part):
    key = jax.random.fold_in(key, 21)
    k_dev, k_round, k_src, k_dst = jax.random.split(key, 4)
    devices = NBLK // BL
    rounds = jnp.arange(BL, dtype=jnp.int32)
    offsets = jnp.where(rounds < CAP, 0, 1 + (rounds - CAP) % max(devices - 1, 1)).astype(jnp.int32)
    offsets = offsets[jax.random.permutation(k_round, BL)]
    owner = jax.random.permutation(k_dev, devices).astype(jnp.int32)
    owner_inv = jnp.argsort(owner).astype(jnp.int32)
    dest = jnp.arange(devices, dtype=jnp.int32)[:, None]
    source = (owner_inv[dest] - offsets[None, :]) % devices
    src_scores = jax.random.randint(k_src, (devices, BL), 0, 1 << 20) * BL + rounds[None, :]
    dst_scores = jax.random.randint(k_dst, (devices, BL), 0, 1 << 20) * BL + rounds[None, :]
    src_order = jnp.argsort(src_scores, axis=1).astype(jnp.int32)
    dst_order = jnp.argsort(dst_scores, axis=1).astype(jnp.int32)
    round_grid = jnp.broadcast_to(rounds[None, :], (devices, BL))
    src_block = source * BL + src_order[source, round_grid]
    dst_block = dest * BL + dst_order
    return jnp.zeros((NBLK,), jnp.int32).at[dst_block.reshape(-1)].set(src_block.reshape(-1).astype(jnp.int32))


def block_levels(stream_key, shape, shards, low, top_value):
    def one(position, shards_of):
        steps = jax.random.uniform(jax.random.fold_in(jax.random.fold_in(stream_key, 6), position), (shards_of,), jnp.float32, low / len(shards), top_value / len(shards))
        return jnp.repeat(jnp.exp(steps), shape[position] // shards_of).reshape((-1,) + (1,) * (len(shape) - position - 1))

    loudness = one(*shards[0])
    for cut in shards[1:]:
        loudness = loudness * one(*cut)
    return loudness


def scatter_about(rng, shape, width, reach, pieces=(), kind=jnp.bfloat16):
    loudness = block_levels(rng, shape, pieces, -0.22, 0.18) if pieces else 1.0
    values = jax.random.normal(rng, shape, jnp.float32) * width * loudness
    return jnp.minimum(jnp.maximum(values, -reach), reach).astype(kind)


def setup_inputs(seed: int = 0) -> dict:
    keys = jax.random.split(jax.random.key(seed), 8)
    acts_a = draw_acts_a(jax.random.fold_in(keys[7], 71), 0)
    acts_b = draw_acts_b(jax.random.fold_in(keys[7], 71), 0)
    grads_a = draw_grads_a(jax.random.fold_in(keys[7], 71), 0)
    grads_b = draw_grads_b(jax.random.fold_in(keys[7], 71), 0)
    weights_a = scatter_about(keys[4], (D, FF), 1.0, 6.0, ((0, 8), (1, 4)))
    weights_b = scatter_about(keys[5], (D, FF), 1.0, 6.0, ((0, 8), (1, 4)))
    block_match = draw_block_match(jax.random.fold_in(keys[7], 71), 0)
    return {"acts_a": acts_a, "acts_b": acts_b, "grads_a": grads_a, "grads_b": grads_b, "weights_a": weights_a, "weights_b": weights_b, "block_match": block_match}


EPSILON = 1e-6


def squared(values):
    wide = values.astype(jnp.float32)
    return (wide * wide).astype(jnp.bfloat16)


def fisher(acts, grads):
    sq_acts = squared(acts).reshape(N_DP, TOK_DEV, D)
    sq_grads = squared(grads).reshape(N_DP, TOK_DEV, FF)

    def add_group(index, total):
        partial_term = jnp.dot(sq_acts[index].T, sq_grads[index], preferred_element_type=jnp.float32)
        return total + partial_term

    return lax.fori_loop(0, N_DP, add_group, jnp.zeros((D, FF), jnp.float32))


def matched(values, block_match):
    return jnp.take(values.reshape(D, NBLK, BLK), block_match, axis=1).reshape(D, FF)


def reference(acts_a, acts_b, grads_a, grads_b, weights_a, weights_b, block_match):
    fisher_a = fisher(acts_a, grads_a)
    fisher_b = matched(fisher(acts_b, grads_b), block_match)
    wide_a = weights_a.astype(jnp.float32)
    wide_b = matched(weights_b, block_match).astype(jnp.float32)
    return (fisher_a * wide_a + fisher_b * wide_b) / (fisher_a + fisher_b + EPSILON)
```

```python
import jax
import jax.numpy as jnp
from jax import lax
from jax.sharding import PartitionSpec as P

BLK = 128
CORES = 2
EPSILON = 1e-06


def squared(values):
    wide = values.astype(jnp.float32)
    return (wide * wide).astype(jnp.bfloat16)


def block_plan(block_match, me, per_dev, capacity, slots):
    total = block_match.shape[0]
    place = jnp.arange(total, dtype=jnp.int32)
    target_dev = place // per_dev
    source_dev = block_match // per_dev
    earlier = (
        (source_dev[:, None] == source_dev[None, :])
        & (target_dev[:, None] == target_dev[None, :])
        & (place[None, :] < place[:, None])
    )
    rank = jnp.sum(earlier.astype(jnp.int32), axis=1)
    out_slot = jnp.where(source_dev == me, target_dev * capacity + rank, -1)
    hits = out_slot[None, :] == jnp.arange(slots, dtype=jnp.int32)[:, None]
    send_block = jnp.sum(jnp.where(hits, (block_match % per_dev)[None, :], 0), axis=1)
    recv_slot = lax.dynamic_slice_in_dim(source_dev * capacity + rank, me * per_dev, per_dev)
    return send_block, recv_slot


def take_blocks(data, ids):
    rows = data.shape[0]
    pieces = [
        lax.dynamic_slice(data, (0, ids[j] * BLK), (rows, BLK)) for j in range(ids.shape[0])
    ]
    return jnp.concatenate(pieces, axis=1)


def match_blocks(data, block_match):
    neurons = lax.axis_size("neuron")
    me = lax.axis_index("neuron")
    per_dev = data.shape[1] // BLK
    capacity = (per_dev + neurons - 1) // neurons
    send_block, recv_slot = block_plan(block_match, me, per_dev, capacity, neurons * capacity)
    rows = data.shape[0]
    width = capacity * BLK
    got = []
    for shift in range(neurons):
        target = (me + shift) % neurons
        ids = lax.dynamic_slice_in_dim(send_block, target * capacity, capacity)
        piece = take_blocks(data, ids)
        if shift:
            piece = lax.ppermute(
                piece, "neuron", [(i, (i + shift) % neurons) for i in range(neurons)]
            )
        got.append(piece)
    received = jnp.concatenate(got, axis=1)
    source = recv_slot // capacity
    place = ((me - source) % neurons) * capacity + recv_slot % capacity
    return take_blocks(received, place)


def gather_acts(acts, chips, inward):
    neurons = lax.axis_size("neuron")
    n_me = lax.axis_index("neuron")
    me = lax.axis_index("dp")
    z, core = me // CORES, me % CORES
    share = acts.shape[0] // neurons
    mine = squared(lax.dynamic_slice_in_dim(acts, n_me * share, share, axis=0)).T
    mine = lax.all_to_all(mine, "dp", split_axis=0, concat_axis=1, tiled=True)
    end = lax.ppermute(mine, "dp", inward)
    both = jnp.concatenate([mine, end], axis=0)
    whole = lax.all_gather(both, "neuron", axis=0)
    sides = []
    for side in range(CORES):
        who = (core + side) % CORES
        groups = []
        for s in range(chips):
            start = (((z - s) % chips) * CORES + who) * share
            groups += [
                lax.dynamic_slice(whole, (n, 0, start), (1, both.shape[0], share))[0]
                for n in range(neurons)
            ]
        sides.append(jnp.concatenate(groups, axis=1))
    return sides


def after(values, *earlier):
    return lax.optimization_barrier((values, *earlier))[0]


def z_pairs(pairs):
    return [(a * CORES + c, b * CORES + c) for a, b in pairs for c in range(CORES)]


def on_device(acts_a, acts_b, grads_a, grads_b, weights_a, weights_b, block_match):
    dp = lax.axis_size("dp")
    chips = dp // CORES
    me = lax.axis_index("dp")
    z = me // CORES
    is_end = (z == 0) | (z == chips - 1)
    rows = weights_a.shape[0]
    tokens = grads_a.shape[0]
    per_dev = grads_a.shape[1] // BLK
    pieces = max(n for n in range(1, 5) if per_dev % n == 0)
    width = grads_a.shape[1] // pieces
    inward = z_pairs([(0, 1), (chips - 1, chips - 2)])
    outward = z_pairs([(1, 0), (chips - 2, chips - 1)])
    swap = [(i, i + 1 - 2 * (i % CORES)) for i in range(dp)]

    def spread(block, inner):
        up, down = block, block
        ups, downs = {}, {}
        skip = 1 if inner else 0
        for hop in range(1, chips - skip):
            up = lax.ppermute(
                up, "dp", z_pairs([(i, i + 1) for i in range(hop - 1, chips - 1 - skip)])
            )
            down = lax.ppermute(
                down, "dp", z_pairs([(i, i - 1) for i in range(1 + skip, chips - hop + 1)])
            )
            ups[hop], downs[hop] = up, down
        slots = [block]
        for s in range(1, chips):
            if s in ups and chips - s in downs:
                slots.append(jnp.where(z >= s, ups[s], downs[chips - s]))
            elif s in ups:
                slots.append(ups[s])
            else:
                slots.append(downs[chips - s])
        held = jnp.concatenate(slots, axis=0)
        return held, lax.ppermute(held, "dp", swap)

    def multiply(sides, pair):
        return sum(
            jnp.dot(side, block, preferred_element_type=jnp.float32)
            for side, block in zip(sides, pair)
        )

    def cut(values, p):
        return values[:, p * width : (p + 1) * width]

    sq_a = squared(grads_a)
    sides = gather_acts(acts_a, chips, inward)
    blocks = [cut(sq_a, p) for p in range(pieces)]
    fishers, totals, sums = [], [], []
    for p in range(2 * pieces):
        block = blocks[p]
        if p >= 2:
            block = after(block, totals[p - 2], *sums[max(p - 3, 0) : p - 2])
        if p == pieces:
            sides = sides_b
        pair = spread(block, p > 0)
        if p == 0:
            total = multiply([side[:rows] for side in sides], pair)
            fishers.append(total)
            sums.append(total)
            totals.append(total)
            late = after((grads_b, weights_b, acts_b), total)
            both_b = jnp.concatenate([squared(late[0]), late[1]], axis=0)
            moved = match_blocks(both_b, block_match)
            sq_b, weights_match = moved[:tokens], moved[tokens:]
            sides_b = gather_acts(late[2], chips, inward)
            blocks += [cut(sq_b, q) for q in range(pieces)]
            continue
        total = multiply(sides, pair)
        totals.append(total)
        sums.append(lax.ppermute(total[rows:], "dp", outward))
        fishers.append(jnp.where(is_end, sums[-1], total[:rows]))
    merged = []
    for p in range(pieces):
        fisher_a, fisher_b = fishers[p], fishers[pieces + p]
        wide_a = cut(weights_a, p).astype(jnp.float32)
        wide_b = cut(weights_match, p).astype(jnp.float32)
        merged.append(
            (fisher_a * wide_a + fisher_b * wide_b) / (fisher_a + fisher_b + EPSILON)
        )
    return jnp.concatenate(merged, axis=1)


def solution(mesh):
    placed = (
        P("dp", None),
        P("dp", None),
        P("dp", "neuron"),
        P("dp", "neuron"),
        P("dp", "neuron"),
        P("dp", "neuron"),
        P(),
    )
    return jax.shard_map(
        on_device, mesh=mesh, in_specs=placed, out_specs=P("dp", "neuron"), check_vma=False
    )
```
